128 devices in a mesh: gx: 16 (over y, z), gy: 8 (over x, core).
Axes of the slice: x: 4, y: 4, z: 4, core: 2. Of those that a mesh axis runs over, the one named last changes fastest.
Arguments:
- queries: bfloat16 [1024, 16384], P('gy', 'gx'), may hold values from -200 to 200, as said below
- keys: bfloat16 [1024, 1024], P('gy'), may hold values from -8 to 8, as said below
- values: bfloat16 [1024, 1024], P('gy'), may hold values from -6 to 6
- lengths: int32 [8], P('gy'), may hold values from 1 to 128, 768 in all
- offsets: int32 [8], P('gy'), may hold values from 0 to 63
- resid_in: bfloat16 [1024, 16384], P('gx', 'gy'), may hold values from -8 to 8, as said below
- w_out: bfloat16 [16384, 16384], P('gx', 'gy'), may hold values from -0.1875 to 0.1875
- norm_gain: bfloat16 [16384], P('gy'), may hold values from 0.5 to 1.5
- w_gate: bfloat16 [16384, 26624], P('gy', 'gx'), may hold values from -0.046875 to 0.046875
- w_up: bfloat16 [16384, 26624], P('gy', 'gx'), may hold values from -0.046875 to 0.046875
- w_down: bfloat16 [26624, 16384], P('gx', 'gy'), may hold values from -0.0390625 to 0.0390625
Outputs:
- layer_out: bfloat16 [1024, 16384], P('gx', 'gy')
The draws below stay inside these ranges and needn't reach their ends.
Inputs may be any that keep to these rules, and one draw needn't show every extreme that they name: queries: some rows may lie along keys of their own sequence. keys are of order one. `resid_in`: entries are of order one.
All inputs are finite; a program needn't handle non-finite values. No bound on the sum of `lengths` on one device may be relied on, other than what follows from the above.
Results may differ from the reference program's by a relative error of at most 0.0055.
Values may be sent and summed in bfloat16 or wider, within the bound.
No kernel may reach another device: no remote copies, remote signals or barrier semaphores. Data moves between devices by JAX's collectives and lax.ppermute only.
A program may use at most 128 MiB of HBM per device.

```python
import math
import jax
import jax.numpy as jnp
import numpy as np
from jax import lax

D = 16384
QUERY_HEADS = 128
KEY_VALUE_HEADS = 8
HEAD_SIZE = 128
FFW = 26624
SEQUENCE_SLOTS = 128
SEQUENCE_COUNT = 8
TOKEN_SLOTS = 1024


def shared_keys(key):
    return jax.random.normal(key, (TOKEN_SLOTS, KEY_VALUE_HEADS * HEAD_SIZE), jnp.float32)


def draw_keys(key, part):
    base_offset = shared_keys(key)
    return jnp.clip(base_offset, -8.0, 8.0).astype(jnp.bfloat16)


def draw_queries(key, part):
    key = jax.random.fold_in(key, 7)
    drawn = jax.random.normal(key, (TOKEN_SLOTS, QUERY_HEADS, HEAD_SIZE), jnp.float32)
    drawn = jnp.clip(drawn, -6.0, 6.0)
    return drawn.reshape(TOKEN_SLOTS, QUERY_HEADS * HEAD_SIZE).astype(jnp.bfloat16)


def column_scales(key, lowest, ratio):
    where = jnp.arange(D, dtype=jnp.float32) / jnp.float32(D - 1)
    jitter = jax.random.uniform(key, (D,), jnp.float32, 0.8, 1.25)
    return lowest * jnp.power(jnp.float32(ratio), where) * jitter


def draw_resid_in(key, part):
    key = jax.random.fold_in(key, 11)
    scale_key = jax.random.fold_in(key, 1)
    entry_key = jax.random.fold_in(key, 2)
    columns = column_scales(scale_key, 0.25, 5.0)
    entries = jnp.clip(jax.random.normal(entry_key, (TOKEN_SLOTS, D), jnp.float32), -6.0, 6.0)
    return jnp.clip(entries * columns[None, :], -8.0, 8.0).astype(jnp.bfloat16)


def plant(values, rng, least, high):
    extent = values.shape
    spot = [jax.random.randint(jax.random.fold_in(rng, axis), (), 0, extent[axis]) for axis in range(len(extent))]
    values = values.at[tuple(spot)].set(least)
    longest = extent.index(max(extent))
    spot[longest] = (spot[longest] + 1) % extent[longest]
    return values.at[tuple(spot)].set(high)


def steps_of(stream_key, shape, shards, least, top_value):
    gain, own = 1.0, jax.random.fold_in(stream_key, 6)
    for position, shards_of in shards:
        heights = jnp.exp(jax.random.uniform(jax.random.fold_in(own, position), (shards_of,), jnp.float32, least / len(shards), top_value / len(shards)))
        gain = gain * jnp.repeat(heights, shape[position] // shards_of).reshape([-1 if axis == position else 1 for axis in range(len(shape))])
    return gain


def split_up(count, total, most, lean):
    weights = [(1 << 20) // math.isqrt(standing ** lean) + 1 for standing in range(2, count + 1)]
    surplus, given = total - most - (count - 1), [1] * (count - 1)
    while surplus > 0:
        candidates = [i for i in range(count - 1) if given[i] < most]
        whole, budget = sum([weights[i] for i in candidates]), surplus
        for i in candidates:
            more = min(most - given[i], max(1, budget * weights[i] // whole), surplus)
            given[i] = given[i] + more
            surplus = surplus - more
    return np.array([most] + given)


def uneven_parts(own_key, amount, total, most, slope):
    if amount == 2:
        one = jax.random.randint(own_key, (), max(1, total - most), min(most, total - 1) + 1)
        return jnp.stack([one, total - one])
    tallies = jnp.asarray(split_up(amount, total, most, slope), jnp.int32)
    couples = (amount - 1) // 2
    giver, taker = tallies[1:1 + 2 * couples:2], tallies[2:2 + 2 * couples:2]
    slack = jnp.minimum(giver - 1, most - taker)
    moved = jax.random.randint(jax.random.fold_in(own_key, 1), (couples,), 0, 1 << 20) % (slack + 1)
    tallies = tallies.at[1:1 + 2 * couples:2].set(giver - moved).at[2:2 + 2 * couples:2].set(taker + moved)
    return tallies[jax.random.permutation(jax.random.fold_in(own_key, 2), amount)]


def centred(key, shape, scale, limit, cuts=(), kind=jnp.bfloat16):
    array = scale * jax.random.normal(key, shape, jnp.float32)
    if cuts:
        array = array * steps_of(key, shape, cuts, -0.22, 0.18)
    return jnp.clip(array, -limit, limit).astype(kind)


def setup_inputs(seed: int = 0) -> dict:
    arg_keys = jax.random.split(jax.random.key(seed), 12)
    queries = draw_queries(jax.random.fold_in(arg_keys[11], 71), 0)
    keys = draw_keys(jax.random.fold_in(arg_keys[11], 71), 0)
    values = centred(arg_keys[2], (TOKEN_SLOTS, KEY_VALUE_HEADS * HEAD_SIZE), 1.0, 6.0, ((0, 8),))
    lengths = uneven_parts(arg_keys[3], SEQUENCE_COUNT, SEQUENCE_COUNT * SEQUENCE_SLOTS * 3 // 4, SEQUENCE_SLOTS, 0).astype(jnp.int32)
    offsets = plant(jax.random.randint(arg_keys[4], (SEQUENCE_COUNT,), 0, SEQUENCE_SLOTS // 2), jax.random.fold_in(arg_keys[4], 1), 0, (SEQUENCE_SLOTS // 2) - 1).astype(jnp.int32)
    resid_in = draw_resid_in(jax.random.fold_in(arg_keys[11], 71), 0)
    w_out = centred(arg_keys[6], (QUERY_HEADS * HEAD_SIZE, D), (QUERY_HEADS * HEAD_SIZE // 16) ** -0.5, 0.1875, ((0, 16), (1, 8)))
    norm_gain = jnp.clip(1.0 + 0.1 * jax.random.normal(arg_keys[7], (D,), jnp.float32), 0.5, 1.5).astype(jnp.bfloat16)
    w_gate = centred(arg_keys[8], (D, FFW), D ** -0.5, 0.046875, ((0, 8), (1, 16)))
    w_up = centred(arg_keys[9], (D, FFW), D ** -0.5, 0.046875, ((0, 8), (1, 16)))
    w_down = centred(arg_keys[10], (FFW, D), FFW ** -0.5, 0.0390625, ((0, 16), (1, 8)))
    return dict(queries=queries, keys=keys, values=values, lengths=lengths, offsets=offsets, resid_in=resid_in, w_out=w_out, norm_gain=norm_gain, w_gate=w_gate, w_up=w_up, w_down=w_down)


def attend(queries, keys, values, lengths, offsets):
    query_group = QUERY_HEADS // KEY_VALUE_HEADS
    query_rows = queries.astype(jnp.float32).reshape(SEQUENCE_COUNT, SEQUENCE_SLOTS, KEY_VALUE_HEADS, query_group, HEAD_SIZE)
    key_rows = keys.astype(jnp.float32).reshape(SEQUENCE_COUNT, SEQUENCE_SLOTS, KEY_VALUE_HEADS, HEAD_SIZE)
    value_rows = values.astype(jnp.float32).reshape(SEQUENCE_COUNT, SEQUENCE_SLOTS, KEY_VALUE_HEADS, HEAD_SIZE)
    scores = jnp.einsum('sqhgd,skhd->shgqk', query_rows, key_rows) / jnp.sqrt(jnp.float32(HEAD_SIZE))
    place = jnp.arange(SEQUENCE_SLOTS, dtype=jnp.int32)
    rows = place[None, :, None]
    cols = place[None, None, :]
    inside = (cols >= offsets[:, None, None]) & (cols < lengths[:, None, None]) & (cols <= rows)
    visible = inside | (cols == rows)
    visible = visible[:, None, None, :, :]
    scores = jnp.where(visible, scores, jnp.float32(-1e+30))
    top = lax.optimization_barrier(jnp.max(scores, axis=-1, keepdims=True))
    expo = jnp.where(visible, jnp.exp(scores - top), jnp.float32(0.0))
    probs = (expo / lax.optimization_barrier(jnp.sum(expo, axis=-1, keepdims=True))).astype(jnp.bfloat16)
    attn = jnp.einsum('shgqk,skhd->sqhgd', probs.astype(jnp.float32), value_rows)
    return attn.astype(jnp.bfloat16).reshape(TOKEN_SLOTS, QUERY_HEADS * HEAD_SIZE)

def reference(queries, keys, values, lengths, offsets, resid_in, w_out, norm_gain, w_gate, w_up, w_down):
    attn = attend(queries, keys, values, lengths, offsets)
    attn_proj = jnp.dot(attn, w_out, preferred_element_type=jnp.float32)
    resid = (resid_in.astype(jnp.float32) + attn_proj).astype(jnp.bfloat16)
    wide = resid.astype(jnp.float32)
    scale = lax.rsqrt(lax.optimization_barrier(jnp.mean(wide * wide, axis=1, keepdims=True)) + 1e-05)
    normed = (wide * scale * norm_gain.astype(jnp.float32)[None, :]).astype(jnp.bfloat16)
    gate = jnp.dot(normed, w_gate, preferred_element_type=jnp.float32)
    up = jnp.dot(normed, w_up, preferred_element_type=jnp.float32)
    hidden = (jax.nn.silu(gate) * up).astype(jnp.bfloat16)
    mixed = jnp.dot(hidden, w_down, preferred_element_type=jnp.float32)
    return (wide + mixed).astype(jnp.bfloat16)
```

```python
import jax
import jax.numpy as jnp
from jax import lax
from jax.sharding import PartitionSpec as P

D = 16384
QUERY_HEADS = 128
KEY_VALUE_HEADS = 8
HEAD_SIZE = 128
SEQUENCE_SLOTS = 128
SIDE = 4
CHUNKS = 1
BF16 = jnp.bfloat16
F32 = jnp.float32

CORES = [[2 * x, 2 * x + 1] for x in range(SIDE)]
SWAP = [(2 * x + c, 2 * x + 1 - c) for x in range(SIDE) for c in range(2)]


def along_y(step):
    return [(4 * y + z, 4 * ((y + step) % 4) + z) for y in range(4) for z in range(4)]


def along_z(step):
    return [(4 * y + z, 4 * y + (z + step) % 4) for y in range(4) for z in range(4)]


def along_x(step):
    return [(2 * x + c, 2 * ((x + step) % 4) + c) for x in range(4) for c in range(2)]


def attend_local(queries, keys, values, lengths, offsets):
    seqs = lengths.shape[0]
    local_heads = queries.shape[1] // HEAD_SIZE
    query_group = QUERY_HEADS // KEY_VALUE_HEADS
    head = lax.axis_index("gx") * local_heads // query_group
    key_one = lax.dynamic_slice_in_dim(keys, head * HEAD_SIZE, HEAD_SIZE, 1).reshape(
        seqs, SEQUENCE_SLOTS, HEAD_SIZE
    )
    value_one = lax.dynamic_slice_in_dim(values, head * HEAD_SIZE, HEAD_SIZE, 1).reshape(
        seqs, SEQUENCE_SLOTS, HEAD_SIZE
    )
    query_all = queries.reshape(seqs, SEQUENCE_SLOTS, local_heads, HEAD_SIZE)
    scores = jnp.einsum("sqhd,skd->shqk", query_all, key_one, preferred_element_type=F32)
    scores = scores / jnp.sqrt(F32(HEAD_SIZE))
    place = jnp.arange(SEQUENCE_SLOTS, dtype=jnp.int32)
    rows = place[None, :, None]
    cols = place[None, None, :]
    inside = (cols >= offsets[:, None, None]) & (cols < lengths[:, None, None]) & (cols <= rows)
    visible = (inside | (cols == rows))[:, None, :, :]
    scores = jnp.where(visible, scores, F32(-1e30))
    top = jnp.max(scores, axis=-1, keepdims=True)
    expo = jnp.where(visible, jnp.exp(scores - top), F32(0.0))
    probs = (expo / jnp.sum(expo, axis=-1, keepdims=True)).astype(BF16)
    attn = jnp.einsum("shqk,skd->sqhd", probs, value_one, preferred_element_type=F32)
    return attn.astype(BF16).reshape(seqs * SEQUENCE_SLOTS, local_heads * HEAD_SIZE)


def pick(array, index, axis=0):
    return lax.dynamic_index_in_dim(array, index, axis, keepdims=False)


def add_up(blocks):
    total = blocks[0].astype(F32)
    for block in blocks[1:]:
        total = total + block.astype(F32)
    return total


def scatter_sum(first, second, at_y, at_z):
    in_y = [lax.ppermute(pick(first, at_y(e)), "gx", along_y(e)) for e in (2, 1, 3)]
    in_z = [lax.ppermute(pick(second, at_z(e), 1), "gx", along_z(e)) for e in (2, 1, 3)]
    first = add_up([pick(first, at_y(0))] + in_y).astype(BF16)
    second = add_up([pick(second, at_z(0), 1)] + in_z).astype(BF16)
    in_z = [lax.ppermute(pick(first, at_z(e)), "gx", along_z(e)) for e in (2, 1, 3)]
    in_y = [lax.ppermute(pick(second, at_y(e)), "gx", along_y(e)) for e in (2, 1, 3)]
    return add_up([pick(first, at_z(0))] + in_z), add_up([pick(second, at_y(0))] + in_y)


def gather(first, second):
    first = jnp.stack([first] + [lax.ppermute(first, "gx", along_z(-e)) for e in (1, 2, 3)])
    second = jnp.stack([second] + [lax.ppermute(second, "gx", along_y(-e)) for e in (1, 2, 3)])
    first = jnp.stack([first] + [lax.ppermute(first, "gx", along_y(-e)) for e in (1, 2, 3)])
    second = jnp.stack([second] + [lax.ppermute(second, "gx", along_z(-e)) for e in (1, 2, 3)], axis=1)
    return first, second


def in_order(core, own, other):
    return jnp.where(core == 0, own, other), jnp.where(core == 0, other, own)


def halves(core, array, axis=0):
    return pick(array, core, axis), pick(array, 1 - core, axis)


def swap(array):
    return lax.ppermute(array, "gy", SWAP)


def both_cores(array, tiled):
    return lax.all_gather(array, "gy", axis=0, tiled=tiled, axis_index_groups=CORES)


def per_device(
    queries, keys, values, lengths, offsets, resid_in, w_out, norm_gain, w_gate, w_up, w_down
):
    place = lax.axis_index("gx")
    y, z = place // SIDE, place % SIDE
    x, core = lax.axis_index("gy") // 2, lax.axis_index("gy") % 2
    rows = resid_in.shape[0] // 2 // CHUNKS
    columns = resid_in.shape[1]

    w_out = both_cores(w_out, False)
    w_gate = both_cores(w_gate, True)
    w_up = both_cores(w_up, True)
    w_down = both_cores(w_down, False)
    gain = jnp.stack(in_order(core, norm_gain, swap(norm_gain))).astype(F32)
    mine, theirs = halves(core, resid_in.reshape(2, CHUNKS, rows, columns))
    resid_in = in_order(core, mine, swap(theirs))

    attn = attend_local(queries, keys, values, lengths, offsets).reshape(2, 2, CHUNKS, rows, -1)
    mine, theirs = halves(core, attn, 1)
    attn_all = jnp.concatenate(in_order(core, mine, swap(theirs)))
    outs = []
    for chunk in range(CHUNKS):
        attn = attn_all[:, chunk]
        attn = jnp.stack([attn] + [lax.ppermute(attn, "gy", along_x(-d)) for d in (1, 2, 3)])
        attn = attn.reshape(16 * rows, -1)
        first, second = [
            jnp.dot(attn, w_out[c], preferred_element_type=F32)
            .astype(BF16)
            .reshape(SIDE, SIDE, rows, columns)
            for c in range(2)
        ]
        sums = scatter_sum(first, second, lambda e: (y + e - x) % 4, lambda e: (z + e) % 4)
        resid = [(resid_in[c][chunk].astype(F32) + sums[c]).astype(BF16) for c in range(2)]
        first, second = [part.reshape(16 * rows, columns).astype(F32) for part in gather(*resid)]
        squares = (jnp.sum(first * first, axis=1) + jnp.sum(second * second, axis=1)).reshape(SIDE, -1)
        scaled = jnp.concatenate(
            [(first * gain[0]).astype(BF16), (second * gain[1]).astype(BF16)], axis=1
        )

        def group(array, d):
            return pick(array, (x + d - y) % 4)

        def over_x(array):
            return add_up(
                [group(array, 0)]
                + [lax.ppermute(group(array, d), "gy", along_x(d)) for d in (2, 1, 3)]
            )

        scale = lax.rsqrt(over_x(squares) / D + 1e-05)[:, None]
        gate, up = [
            over_x(
                jnp.dot(scaled, weight, preferred_element_type=F32)
                .astype(BF16)
                .reshape(SIDE, SIDE * rows, -1)
            )
            * scale
            for weight in (w_gate, w_up)
        ]
        hidden = (jax.nn.silu(gate) * up).astype(BF16)
        hidden = jnp.stack([hidden] + [lax.ppermute(hidden, "gy", along_x(-d)) for d in (1, 2, 3)])
        hidden = hidden.reshape(16 * rows, -1)
        first, second = [
            jnp.dot(hidden, w_down[c], preferred_element_type=F32)
            .astype(BF16)
            .reshape(SIDE, SIDE, rows, columns)
            for c in range(2)
        ]
        sums = scatter_sum(first, second, lambda e: (y + e - x) % 4, lambda e: e)
        outs.append([(resid[c].astype(F32) + sums[c]).astype(BF16) for c in range(2)])
    outs = jnp.stack([jnp.concatenate([out[c] for out in outs]) for c in range(2)])
    mine, theirs = halves(core, outs)
    return jnp.concatenate(in_order(core, mine, swap(theirs)))


def solution(mesh):
    in_specs = (
        P("gy", "gx"),
        P("gy", None),
        P("gy", None),
        P("gy"),
        P("gy"),
        P("gx", "gy"),
        P("gx", "gy"),
        P("gy"),
        P("gy", "gx"),
        P("gy", "gx"),
        P("gx", "gy"),
    )
    out_specs = P("gx", "gy")
    return jax.shard_map(
        per_device, mesh=mesh, in_specs=in_specs, out_specs=out_specs, check_vma=False
    )
```

```python
import jax
import jax.numpy as jnp
from jax import lax
from jax.experimental import pallas as pl
from jax.experimental.pallas import tpu as pltpu
from jax.sharding import PartitionSpec as P

D = 16384
QUERY_HEADS = 128
KEY_VALUE_HEADS = 8
HEAD_SIZE = 128
SEQUENCE_SLOTS = 128
SIDE = 4
TILE = 256
AHEAD = 6
VMEM_BYTES = 52 * 1024 * 1024
BF16 = jnp.bfloat16
F32 = jnp.float32

BOTH = ("gx", "gy")
CORES = [[2 * x, 2 * x + 1] for x in range(SIDE)]
SWAP = [(2 * x + c, 2 * x + 1 - c) for x in range(SIDE) for c in range(2)]


def across(major, mask):
    pairs = []
    for place in range(16):
        for spot in range(8):
            flip = mask if (spot % 2 == 0) == major else 4 * mask
            pairs.append((8 * place + spot, 8 * (place ^ flip) + spot))
    return pairs


def across_x(masks):
    return [(spot, spot ^ (2 * masks[spot % 2])) for spot in range(8)]


def attend_local(queries, keys, values, lengths, offsets):
    seqs = lengths.shape[0]
    local_heads = queries.shape[1] // HEAD_SIZE
    query_group = QUERY_HEADS // KEY_VALUE_HEADS
    head = lax.axis_index("gx") * local_heads // query_group
    key_one = lax.dynamic_slice_in_dim(keys, head * HEAD_SIZE, HEAD_SIZE, 1).reshape(
        seqs, SEQUENCE_SLOTS, HEAD_SIZE
    )
    value_one = lax.dynamic_slice_in_dim(values, head * HEAD_SIZE, HEAD_SIZE, 1).reshape(
        seqs, SEQUENCE_SLOTS, HEAD_SIZE
    )
    query_all = queries.reshape(seqs, SEQUENCE_SLOTS, local_heads, HEAD_SIZE)
    scores = jnp.einsum("sqhd,skd->shqk", query_all, key_one, preferred_element_type=F32)
    scores = scores / jnp.sqrt(F32(HEAD_SIZE))
    place = jnp.arange(SEQUENCE_SLOTS, dtype=jnp.int32)
    rows = place[None, :, None]
    cols = place[None, None, :]
    inside = (cols >= offsets[:, None, None]) & (cols < lengths[:, None, None]) & (cols <= rows)
    visible = (inside | (cols == rows))[:, None, :, :]
    scores = jnp.where(visible, scores, F32(-1e30))
    top = jnp.max(scores, axis=-1, keepdims=True)
    expo = jnp.where(visible, jnp.exp(scores - top), F32(0.0))
    probs = (expo / jnp.sum(expo, axis=-1, keepdims=True)).astype(BF16)
    attn = jnp.einsum("shqk,skd->sqhd", probs, value_one, preferred_element_type=F32)
    return attn.astype(BF16).reshape(seqs * SEQUENCE_SLOTS, local_heads * HEAD_SIZE)


def pick(array, index, axis=0):
    return lax.dynamic_index_in_dim(array, index, axis, keepdims=False)


def add_up(blocks):
    total = blocks[0].astype(F32)
    for block in blocks[1:]:
        total = total + block.astype(F32)
    return total


def move(array, major, mask):
    return lax.ppermute(array, BOTH, across(major, mask))


def sum_major(blocks, size):
    blocks = [blocks[0]] + [move(blocks[e], True, e) for e in (2, 1, 3)]
    return [add_up([block[q * size : (q + 1) * size] for block in blocks]) for q in range(SIDE)]


def gather_x(block):
    other = lax.ppermute(block, "gy", across_x((1, 3)))
    return [block, other, lax.ppermute(jnp.concatenate([block, other]), "gy", across_x((3, 1)))]


def halves(core, array, axis=0):
    return pick(array, core, axis), pick(array, 1 - core, axis)


def swap(array):
    return lax.ppermute(array, "gy", SWAP)


def in_three(sums):
    lanes = []
    for _ in range(3):
        rounded = lax.reduce_precision(sums, 8, 7)
        lanes.append(rounded.astype(BF16))
        sums = sums - rounded
    return jnp.pad(jnp.stack(lanes, axis=1), ((0, 0), (0, 128 - 3)))


def after(array, *earlier):
    return lax.optimization_barrier((array, earlier))[0]


SMEM = pl.BlockSpec(memory_space=pltpu.SMEM)
VMEM = pl.BlockSpec(memory_space=pltpu.VMEM)
HBM = pl.BlockSpec(memory_space=pltpu.HBM)


def fill(places, given, lhs, size):
    i = 0
    for ref in given:
        for row in range(0, ref.shape[0], size):
            at = pl.multiple_of(places[i] * size, size)
            lhs[pl.ds(at, size), :] = ref[row : row + size, :]
            i += 1


def project(places, size, blocks, weight):
    depth, width = weight.shape
    rows = size * places.shape[0]
    tiles = width // TILE

    def kernel(places, *refs):
        given, weight_ref, outs = refs[: len(blocks)], refs[-8], refs[-7:-3]
        lhs, tile_refs, sems = refs[-3:]

        def copy(j):
            at = pl.ds(pl.multiple_of(j * TILE, TILE), TILE)
            return pltpu.make_async_copy(weight_ref.at[:, at], tile_refs.at[j], sems.at[j])

        for j in range(tiles):
            copy(j).start()
        fill(places, given, lhs, size)

        @pl.loop(0, tiles)
        def _(j):
            copy(j).wait()
            product = jnp.dot(lhs[...], tile_refs[j], preferred_element_type=F32).astype(BF16)
            at = pl.ds(pl.multiple_of(j * TILE, TILE), TILE)
            for e in range(4):
                outs[e][:, at] = product[e * rows // 4 : (e + 1) * rows // 4]

    return pl.pallas_call(
        kernel,
        in_specs=[SMEM] + [VMEM] * len(blocks) + [HBM],
        out_specs=[VMEM] * 4,
        scratch_shapes=[
            pltpu.VMEM((rows, depth), BF16),
            pltpu.VMEM((tiles, depth, TILE), BF16),
            pltpu.SemaphoreType.DMA((tiles,)),
        ],
        out_shape=[jax.ShapeDtypeStruct((rows // 4, width), BF16)] * 4,
        compiler_params=pltpu.CompilerParams(vmem_limit_bytes=VMEM_BYTES),
        cost_estimate=pl.CostEstimate(
            flops=2 * rows * depth * width, bytes_accessed=2 * depth * width, transcendentals=0
        ),
    )(places, *blocks, weight)


def gate_and_up(places, blocks, w_gate, w_up):
    depth, units = w_gate.shape
    rows = blocks[0].shape[0]
    full = units // TILE
    rest = units - full * TILE

    def kernel(places, *refs):
        given, gate_ref, up_ref, outs = refs[:4], refs[4], refs[5], refs[6:8]
        lhs, tile_refs, sems = refs[8:]

        def copy(weight_ref, j, first):
            at = pl.ds(pl.multiple_of(j * TILE, TILE), TILE)
            return pltpu.make_async_copy(
                weight_ref.at[:, at], tile_refs.at[first + j], sems.at[first + j]
            )

        def copy_rest(weight_ref, i):
            return pltpu.make_async_copy(
                weight_ref.at[:, pl.ds(full * TILE, rest)],
                tile_refs.at[2 * full, :, pl.ds(i * rest, rest)],
                sems.at[2 * full + i],
            )

        def store(product, at):
            for i in range(2):
                outs[i][:, at] = product[2 * i * rows : 2 * (i + 1) * rows]

        def multiply(tile):
            return jnp.dot(lhs[:, :depth], tile, preferred_element_type=F32).astype(BF16)

        for j in range(AHEAD):
            copy(gate_ref, j, 0).start()
        fill(places, given, lhs, rows)
        store(lhs[:, depth:], pl.ds(2 * units, 128))

        @pl.loop(0, full)
        def _(j):
            copy(gate_ref, j, 0).wait()

            @pl.when(j + AHEAD < full)
            def _():
                copy(gate_ref, j + AHEAD, 0).start()

            @pl.when(j + AHEAD >= full)
            def _():
                copy(up_ref, j + AHEAD - full, full).start()

            at = pl.multiple_of(j * TILE, TILE)
            store(multiply(tile_refs[j]), pl.ds(at, TILE))

        @pl.loop(0, full)
        def _(j):
            copy(up_ref, j, full).wait()

            @pl.when(j + AHEAD < full)
            def _():
                copy(up_ref, j + AHEAD, full).start()

            @pl.when(j + AHEAD == full)
            def _():
                copy_rest(gate_ref, 0).start()
                copy_rest(up_ref, 1).start()

            at = pl.multiple_of(units + j * TILE, 128)
            store(multiply(tile_refs[full + j]), pl.ds(at, TILE))

        copy_rest(gate_ref, 0).wait()
        copy_rest(up_ref, 1).wait()
        product = multiply(tile_refs[2 * full])
        store(product[:, :rest], pl.ds(full * TILE, rest))
        store(product[:, rest:], pl.ds(units + full * TILE, rest))

    return pl.pallas_call(
        kernel,
        in_specs=[SMEM] + [VMEM] * 4 + [HBM] * 2,
        out_specs=[VMEM] * 2,
        scratch_shapes=[
            pltpu.VMEM((4 * rows, depth + 128), BF16),
            pltpu.VMEM((2 * full + 1, depth, TILE), BF16),
            pltpu.SemaphoreType.DMA((2 * full + 2,)),
        ],
        out_shape=[jax.ShapeDtypeStruct((2 * rows, 2 * units + 128), BF16)] * 2,
        compiler_params=pltpu.CompilerParams(vmem_limit_bytes=VMEM_BYTES),
        cost_estimate=pl.CostEstimate(
            flops=16 * rows * depth * units, bytes_accessed=4 * depth * units, transcendentals=0
        ),
    )(places, *blocks, w_gate, w_up)


def sum_over_x(sent, kept, earlier):
    rows = sent.shape[0] // 2
    arrived = lax.ppermute(sent, "gy", across_x((3, 1)))
    other = (kept[rows:].astype(F32) + arrived[rows:].astype(F32)).astype(BF16)
    if earlier is not None:
        other = after(other, earlier)
    other = lax.ppermute(other, "gy", across_x((1, 3)))
    return add_up([kept[:rows], arrived[:rows], other])


def per_device(
    queries, keys, values, lengths, offsets, resid_in, w_out, norm_gain, w_gate, w_up, w_down
):
    place = lax.axis_index("gx")
    y, z = place // SIDE, place % SIDE
    x, core = lax.axis_index("gy") // 2, lax.axis_index("gy") % 2
    here, there = jnp.where(core == 0, z, y), jnp.where(core == 0, y, z)
    rows, columns = resid_in.shape
    half = rows // 2
    units = w_gate.shape[1]
    four = jnp.arange(SIDE, dtype=jnp.int32)
    two = jnp.arange(2, dtype=jnp.int32)
    cores = jnp.stack([core, 1 - core])

    w_gate = lax.all_gather(w_gate, "gy", axis=0, tiled=True, axis_index_groups=CORES)
    w_up = lax.all_gather(w_up, "gy", axis=0, tiled=True, axis_index_groups=CORES)

    mine = attend_local(queries, keys, values, lengths, offsets)
    mine = gather_x(mine)
    theirs = swap(jnp.concatenate(mine))
    near = jnp.where(core == 0, 1, 3)
    zero, far = jnp.zeros_like(near), jnp.full_like(near, 2)
    lines = x ^ jnp.stack(
        [
            jnp.stack([zero, near, 4 - near, far]),
            jnp.stack([zero, 4 - near, near, far]),
        ]
    )
    in_y = (lines ^ y)[:, :, None]
    in_z = ((2 * cores[:, None] + two[None, :]) ^ z)[:, None, :]
    places = jnp.where(core == 0, 4 * in_z + in_y, 4 * in_y + in_z).reshape(16)
    parts = sum_major(project(places, rows, mine + [theirs], w_out), rows)
    arrived = [move(parts[q].astype(BF16), False, q) for q in (2, 1, 3)]
    attn_proj = add_up([parts[0]] + arrived)
    wide = (resid_in.astype(F32) + attn_proj).astype(BF16).astype(F32)
    squares = in_three(jnp.sum(wide * wide, axis=1))
    scaled = jnp.concatenate([(wide * norm_gain.astype(F32)).astype(BF16), squares], axis=1)
    mine, theirs = halves(core, scaled.reshape(2, half, -1))
    theirs = swap(theirs)
    first, second = jnp.where(core == 0, mine, theirs), jnp.where(core == 0, theirs, mine)
    squares = mine[:, columns:].astype(F32) + theirs[:, columns:].astype(F32)
    scaled = jnp.concatenate(
        [first[:, :columns], second[:, :columns], in_three(jnp.sum(squares, axis=1))], axis=1
    )
    scaled = [scaled] + [move(scaled, False, q) for q in (1, 2, 3)]

    quarter = half // 2
    outs, hidden = [], None
    for chunk in range(2):
        taken = slice(chunk * quarter, (chunk + 1) * quarter)
        block = jnp.concatenate([block[taken] for block in scaled])
        blocks = [block] + [move(block, True, e) for e in (1, 2, 3)]
        slot = x ^ here ^ four
        slots = jnp.where(slot == 4 - near, 0, jnp.where(slot == 2, 1, jnp.where(slot == 0, 2, 3)))
        both = sum_over_x(*gate_and_up(slots, blocks, w_gate, w_up), hidden)
        scale = lax.rsqrt(jnp.sum(both[:, 2 * units :], axis=1, keepdims=True) / D + 1e-05)
        gate, up = both[:, :units] * scale, both[:, units : 2 * units] * scale
        hidden = (jax.nn.silu(gate) * up).astype(BF16)
        mine = gather_x(hidden)
        if chunk:
            mine = after(mine, *products)
        theirs = swap(jnp.concatenate(mine))
        ours = 4 * (lines[0] ^ here)[:, None] + four[None, :]
        others = (lines[1] ^ there)[:, None] + 4 * four[None, :]
        places = jnp.stack([2 * ours + core, 2 * others + 1 - core]).reshape(32)
        products = project(places, quarter, mine + [theirs], w_down)
        parts = sum_major(products, half)
        arrived = [move(parts[q].astype(BF16), False, q) for q in (2, 1, 3)]
        own = wide.reshape(2, 2, quarter, columns)[:, chunk].reshape(half, columns)
        outs.append((own + add_up([parts[0]] + arrived)).astype(BF16).reshape(2, quarter, columns))
    return jnp.stack(outs, axis=1).reshape(rows, columns)


def solution(mesh):
    in_specs = (
        P("gy", "gx"),
        P("gy", None),
        P("gy", None),
        P("gy"),
        P("gy"),
        P("gx", "gy"),
        P("gx", "gy"),
        P("gy"),
        P("gy", "gx"),
        P("gy", "gx"),
        P("gx", "gy"),
    )
    out_specs = P("gx", "gy")
    return jax.shard_map(
        per_device, mesh=mesh, in_specs=in_specs, out_specs=out_specs, check_vma=False
    )
```

```python
import jax
import jax.numpy as jnp
from jax import lax
from jax.experimental import pallas as pl
from jax.experimental.pallas import tpu as pltpu
from jax.sharding import PartitionSpec as P

D = 16384
QUERY_HEADS = 128
KEY_VALUE_HEADS = 8
HEAD_SIZE = 128
SEQUENCE_SLOTS = 128
SIDE = 4
TILE = 256
AHEAD = 6
PIECES = 8
PROJECT_BYTES = 12 * 1024 * 1024
VMEM_BYTES = 52 * 1024 * 1024
BF16 = jnp.bfloat16
F32 = jnp.float32

BOTH = ("gx", "gy")
CORES = [[2 * x, 2 * x + 1] for x in range(SIDE)]
SWAP = [(2 * x + c, 2 * x + 1 - c) for x in range(SIDE) for c in range(2)]


def across(major, mask):
    pairs = []
    for place in range(16):
        for spot in range(8):
            flip = mask if (spot % 2 == 0) == major else 4 * mask
            pairs.append((8 * place + spot, 8 * (place ^ flip) + spot))
    return pairs


def across_x(masks):
    return [(spot, spot ^ (2 * masks[spot % 2])) for spot in range(8)]


def attend_local(queries, keys, values, lengths, offsets):
    seqs = lengths.shape[0]
    local_heads = queries.shape[1] // HEAD_SIZE
    query_group = QUERY_HEADS // KEY_VALUE_HEADS
    head = lax.axis_index("gx") * local_heads // query_group
    key_one = lax.dynamic_slice_in_dim(keys, head * HEAD_SIZE, HEAD_SIZE, 1).reshape(
        seqs, SEQUENCE_SLOTS, HEAD_SIZE
    )
    value_one = lax.dynamic_slice_in_dim(values, head * HEAD_SIZE, HEAD_SIZE, 1).reshape(
        seqs, SEQUENCE_SLOTS, HEAD_SIZE
    )
    query_all = queries.reshape(seqs, SEQUENCE_SLOTS, local_heads, HEAD_SIZE)
    scores = jnp.einsum("sqhd,skd->shqk", query_all, key_one, preferred_element_type=F32)
    scores = scores / jnp.sqrt(F32(HEAD_SIZE))
    place = jnp.arange(SEQUENCE_SLOTS, dtype=jnp.int32)
    rows = place[None, :, None]
    cols = place[None, None, :]
    inside = (cols >= offsets[:, None, None]) & (cols < lengths[:, None, None]) & (cols <= rows)
    visible = (inside | (cols == rows))[:, None, :, :]
    scores = jnp.where(visible, scores, F32(-1e30))
    top = jnp.max(scores, axis=-1, keepdims=True)
    expo = jnp.where(visible, jnp.exp(scores - top), F32(0.0))
    probs = (expo / jnp.sum(expo, axis=-1, keepdims=True)).astype(BF16)
    attn = jnp.einsum("shqk,skd->sqhd", probs, value_one, preferred_element_type=F32)
    return attn.astype(BF16).reshape(seqs * SEQUENCE_SLOTS, local_heads * HEAD_SIZE)


def pick(array, index, axis=0):
    return lax.dynamic_index_in_dim(array, index, axis, keepdims=False)


def add_up(blocks):
    total = blocks[0].astype(F32)
    for block in blocks[1:]:
        total = total + block.astype(F32)
    return total


def move(array, major, mask):
    return lax.ppermute(array, BOTH, across(major, mask))


def sum_major(blocks, size):
    blocks = [blocks[0]] + [move(blocks[e], True, e) for e in (2, 1, 3)]
    return [add_up([block[q * size : (q + 1) * size] for block in blocks]) for q in range(SIDE)]


def gather_x(block, earlier=None):
    other = lax.ppermute(block, "gy", across_x((1, 3)))
    if earlier is not None:
        other = after(other, earlier)
    return [block, other, lax.ppermute(jnp.concatenate([block, other]), "gy", across_x((3, 1)))]


def halves(core, array, axis=0):
    return pick(array, core, axis), pick(array, 1 - core, axis)


def swap(array):
    return lax.ppermute(array, "gy", SWAP)


def in_three(sums):
    lanes = []
    for _ in range(3):
        rounded = lax.reduce_precision(sums, 8, 7)
        lanes.append(rounded.astype(BF16))
        sums = sums - rounded
    return jnp.pad(jnp.stack(lanes, axis=1), ((0, 0), (0, 128 - 3)))


def after(array, *earlier):
    return lax.optimization_barrier((array, earlier))[0]


SMEM = pl.BlockSpec(memory_space=pltpu.SMEM)
VMEM = pl.BlockSpec(memory_space=pltpu.VMEM)
HBM = pl.BlockSpec(memory_space=pltpu.HBM)


def fill(places, given, lhs, size):
    i = 0
    for ref in given:
        for row in range(0, ref.shape[0], size):
            at = pl.multiple_of(places[i] * size, size)
            lhs[pl.ds(at, size), :] = ref[row : row + size, :]
            i += 1


def start_all(sources, targets, sems):
    copies = []
    for source, target in zip(sources, targets):
        piece = source.shape[0] // PIECES
        for j in range(PIECES):
            at = pl.ds(j * piece, piece)
            copies.append(
                pltpu.make_async_copy(source.at[at], target.at[at], sems.at[len(copies)])
            )
    for copy in copies:
        copy.start()
    return copies


def load(*weights):
    count = len(weights)

    def kernel(*refs):
        for copy in start_all(refs[:count], refs[count : 2 * count], refs[-1]):
            copy.wait()

    return pl.pallas_call(
        kernel,
        in_specs=[HBM] * count,
        out_specs=[VMEM] * count,
        scratch_shapes=[pltpu.SemaphoreType.DMA((count * PIECES,))],
        out_shape=[jax.ShapeDtypeStruct(weight.shape, BF16) for weight in weights],
        compiler_params=pltpu.CompilerParams(vmem_limit_bytes=PROJECT_BYTES),
        cost_estimate=pl.CostEstimate(
            flops=0, bytes_accessed=sum(2 * weight.size for weight in weights), transcendentals=0
        ),
    )(*weights)


def project(places, size, blocks, weight):
    depth, width = weight.shape
    rows = size * places.shape[0]

    def kernel(places, *refs):
        given, weight_ref, outs, lhs = refs[: len(blocks)], refs[-6], refs[-5:-1], refs[-1]
        fill(places, given, lhs, size)
        for first in range(0, width, TILE):
            at = pl.ds(first, TILE)
            product = jnp.dot(lhs[...], weight_ref[:, at], preferred_element_type=F32).astype(BF16)
            for e in range(4):
                outs[e][:, at] = product[e * rows // 4 : (e + 1) * rows // 4]

    return pl.pallas_call(
        kernel,
        in_specs=[SMEM] + [VMEM] * (len(blocks) + 1),
        out_specs=[VMEM] * 4,
        scratch_shapes=[pltpu.VMEM((rows, depth), BF16)],
        out_shape=[jax.ShapeDtypeStruct((rows // 4, width), BF16)] * 4,
        compiler_params=pltpu.CompilerParams(vmem_limit_bytes=PROJECT_BYTES),
        cost_estimate=pl.CostEstimate(
            flops=2 * rows * depth * width, bytes_accessed=2 * depth * width, transcendentals=0
        ),
    )(places, *blocks, weight)


def gate_and_up(places, blocks, w_gate, w_up):
    depth, units = w_gate.shape
    rows = blocks[0].shape[0]
    full = units // TILE
    rest = units - full * TILE

    def kernel(places, *refs):
        given, gate_ref, up_ref, outs = refs[:4], refs[4], refs[5], refs[6:8]
        lhs, tile_refs, sems = refs[8:]

        def copy(weight_ref, j, first):
            at = pl.ds(pl.multiple_of(j * TILE, TILE), TILE)
            return pltpu.make_async_copy(
                weight_ref.at[:, at], tile_refs.at[first + j], sems.at[first + j]
            )

        def copy_rest(weight_ref, i):
            return pltpu.make_async_copy(
                weight_ref.at[:, pl.ds(full * TILE, rest)],
                tile_refs.at[2 * full, :, pl.ds(i * rest, rest)],
                sems.at[2 * full + i],
            )

        def store(product, at):
            for i in range(2):
                outs[i][:, at] = product[2 * i * rows : 2 * (i + 1) * rows]

        def multiply(tile):
            return jnp.dot(lhs[:, :depth], tile, preferred_element_type=F32).astype(BF16)

        for j in range(AHEAD):
            copy(gate_ref, j, 0).start()
        fill(places, given, lhs, rows)
        store(lhs[:, depth:], pl.ds(2 * units, 128))

        @pl.loop(0, full)
        def _(j):
            copy(gate_ref, j, 0).wait()

            @pl.when(j + AHEAD < full)
            def _():
                copy(gate_ref, j + AHEAD, 0).start()

            @pl.when(j + AHEAD >= full)
            def _():
                copy(up_ref, j + AHEAD - full, full).start()

            at = pl.multiple_of(j * TILE, TILE)
            store(multiply(tile_refs[j]), pl.ds(at, TILE))

        @pl.loop(0, full)
        def _(j):
            copy(up_ref, j, full).wait()

            @pl.when(j + AHEAD < full)
            def _():
                copy(up_ref, j + AHEAD, full).start()

            @pl.when(j + AHEAD == full)
            def _():
                copy_rest(gate_ref, 0).start()
                copy_rest(up_ref, 1).start()

            at = pl.multiple_of(units + j * TILE, 128)
            store(multiply(tile_refs[full + j]), pl.ds(at, TILE))

        copy_rest(gate_ref, 0).wait()
        copy_rest(up_ref, 1).wait()
        product = multiply(tile_refs[2 * full])
        store(product[:, :rest], pl.ds(full * TILE, rest))
        store(product[:, rest:], pl.ds(units + full * TILE, rest))

    return pl.pallas_call(
        kernel,
        in_specs=[SMEM] + [VMEM] * 4 + [HBM] * 2,
        out_specs=[VMEM] * 2,
        scratch_shapes=[
            pltpu.VMEM((4 * rows, depth + 128), BF16),
            pltpu.VMEM((2 * full + 1, depth, TILE), BF16),
            pltpu.SemaphoreType.DMA((2 * full + 2,)),
        ],
        out_shape=[jax.ShapeDtypeStruct((2 * rows, 2 * units + 128), BF16)] * 2,
        compiler_params=pltpu.CompilerParams(vmem_limit_bytes=VMEM_BYTES),
        cost_estimate=pl.CostEstimate(
            flops=16 * rows * depth * units, bytes_accessed=4 * depth * units, transcendentals=0
        ),
    )(places, *blocks, w_gate, w_up)


def sum_over_x(sent, kept, earlier):
    rows = sent.shape[0] // 2
    arrived = after(lax.ppermute(sent, "gy", across_x((3, 1))), earlier)
    other = (kept[rows:].astype(F32) + arrived[rows:].astype(F32)).astype(BF16)
    other = lax.ppermute(other, "gy", across_x((1, 3)))
    return add_up([kept[:rows], arrived[:rows], other])


def per_device(
    queries, keys, values, lengths, offsets, resid_in, w_out, norm_gain, w_gate, w_up, w_down
):
    place = lax.axis_index("gx")
    y, z = place // SIDE, place % SIDE
    x, core = lax.axis_index("gy") // 2, lax.axis_index("gy") % 2
    here, there = jnp.where(core == 0, z, y), jnp.where(core == 0, y, z)
    rows, columns = resid_in.shape
    half = rows // 2
    units = w_gate.shape[1]
    four = jnp.arange(SIDE, dtype=jnp.int32)
    two = jnp.arange(2, dtype=jnp.int32)
    cores = jnp.stack([core, 1 - core])

    w_gate = lax.all_gather(w_gate, "gy", axis=0, tiled=True, axis_index_groups=CORES)
    w_up = lax.all_gather(w_up, "gy", axis=0, tiled=True, axis_index_groups=CORES)

    mine = attend_local(queries, keys, values, lengths, offsets)
    (out_weight,) = load(after(w_out, mine))
    mine = gather_x(mine, out_weight)
    theirs = swap(jnp.concatenate(mine))
    near = jnp.where(core == 0, 1, 3)
    zero, far = jnp.zeros_like(near), jnp.full_like(near, 2)
    lines = x ^ jnp.stack(
        [
            jnp.stack([zero, near, 4 - near, far]),
            jnp.stack([zero, 4 - near, near, far]),
        ]
    )
    in_y = (lines ^ y)[:, :, None]
    in_z = ((2 * cores[:, None] + two[None, :]) ^ z)[:, None, :]
    places = jnp.where(core == 0, 4 * in_z + in_y, 4 * in_y + in_z).reshape(16)
    parts = sum_major(project(places, rows, mine + [theirs], out_weight), rows)
    arrived = [move(parts[q].astype(BF16), False, q) for q in (2, 1, 3)]
    attn_proj = add_up([parts[0]] + arrived)
    wide = (resid_in.astype(F32) + attn_proj).astype(BF16).astype(F32)
    squares = in_three(jnp.sum(wide * wide, axis=1))
    scaled = jnp.concatenate([(wide * norm_gain.astype(F32)).astype(BF16), squares], axis=1)
    mine, theirs = halves(core, scaled.reshape(2, half, -1))
    theirs = swap(theirs)
    first, second = jnp.where(core == 0, mine, theirs), jnp.where(core == 0, theirs, mine)
    squares = mine[:, columns:].astype(F32) + theirs[:, columns:].astype(F32)
    scaled = jnp.concatenate(
        [first[:, :columns], second[:, :columns], in_three(jnp.sum(squares, axis=1))], axis=1
    )
    scaled = [scaled] + [move(scaled, False, q) for q in (1, 2, 3)]

    quarter = half // 2
    slot = x ^ here ^ four
    slots = jnp.where(slot == 4 - near, 0, jnp.where(slot == 2, 1, jnp.where(slot == 0, 2, 3)))
    products = []
    for chunk in range(2):
        taken = slice(chunk * quarter, (chunk + 1) * quarter)
        block = jnp.concatenate([block[taken] for block in scaled])
        blocks = [block] + [move(block, True, e) for e in (1, 2, 3)]
        products.append(gate_and_up(slots, blocks, w_gate, w_up))
    outs, placed = [], None
    for chunk, (sent, kept) in enumerate(products):
        both = sum_over_x(sent, kept, hidden if chunk else products[1][0])
        if not chunk:
            (down_weight,) = load(after(w_down, products[1][0]))
            both = after(both, down_weight)
        scale = lax.rsqrt(jnp.sum(both[:, 2 * units :], axis=1, keepdims=True) / D + 1e-05)
        gate, up = both[:, :units] * scale, both[:, units : 2 * units] * scale
        hidden = (jax.nn.silu(gate) * up).astype(BF16)
        mine = gather_x(hidden)
        if chunk:
            mine = after(mine, *placed)
        theirs = swap(jnp.concatenate(mine))
        ours = 4 * (lines[0] ^ here)[:, None] + four[None, :]
        others = (lines[1] ^ there)[:, None] + 4 * four[None, :]
        places = jnp.stack([2 * ours + core, 2 * others + 1 - core]).reshape(32)
        placed = project(places, quarter, mine + [theirs], down_weight)
        parts = sum_major(placed, half)
        arrived = [move(parts[q].astype(BF16), False, q) for q in (2, 1, 3)]
        own = wide.reshape(2, 2, quarter, columns)[:, chunk].reshape(half, columns)
        outs.append((own + add_up([parts[0]] + arrived)).astype(BF16).reshape(2, quarter, columns))
    return jnp.stack(outs, axis=1).reshape(rows, columns)


def solution(mesh):
    in_specs = (
        P("gy", "gx"),
        P("gy", None),
        P("gy", None),
        P("gy"),
        P("gy"),
        P("gx", "gy"),
        P("gx", "gy"),
        P("gy"),
        P("gy", "gx"),
        P("gy", "gx"),
        P("gx", "gy"),
    )
    out_specs = P("gx", "gy")
    return jax.shard_map(
        per_device, mesh=mesh, in_specs=in_specs, out_specs=out_specs, check_vma=False
    )
```

```python
import jax
import jax.numpy as jnp
from jax import lax
from jax.experimental import pallas as pl
from jax.experimental.pallas import tpu as pltpu
from jax.sharding import PartitionSpec as P

D = 16384
QUERY_HEADS = 128
KEY_VALUE_HEADS = 8
HEAD_SIZE = 128
SEQUENCE_SLOTS = 128
SIDE = 4
TILE = 256
AHEAD = 2
WIDE = 512
PIECES = 8
PROJECT_BYTES = 12 * 1024 * 1024
VMEM_BYTES = 52 * 1024 * 1024
BF16 = jnp.bfloat16
F32 = jnp.float32

BOTH = ("gx", "gy")
CORES = [[2 * x, 2 * x + 1] for x in range(SIDE)]
SWAP = [(2 * x + c, 2 * x + 1 - c) for x in range(SIDE) for c in range(2)]


def across(major, mask):
    pairs = []
    for place in range(16):
        for spot in range(8):
            flip = mask if (spot % 2 == 0) == major else 4 * mask
            pairs.append((8 * place + spot, 8 * (place ^ flip) + spot))
    return pairs


def across_x(masks):
    return [(spot, spot ^ (2 * masks[spot % 2])) for spot in range(8)]


def attend_local(queries, keys, values, lengths, offsets):
    seqs = lengths.shape[0]
    local_heads = queries.shape[1] // HEAD_SIZE
    query_group = QUERY_HEADS // KEY_VALUE_HEADS
    head = lax.axis_index("gx") * local_heads // query_group
    key_one = lax.dynamic_slice_in_dim(keys, head * HEAD_SIZE, HEAD_SIZE, 1).reshape(
        seqs, SEQUENCE_SLOTS, HEAD_SIZE
    )
    value_one = lax.dynamic_slice_in_dim(values, head * HEAD_SIZE, HEAD_SIZE, 1).reshape(
        seqs, SEQUENCE_SLOTS, HEAD_SIZE
    )
    query_all = queries.reshape(seqs, SEQUENCE_SLOTS, local_heads, HEAD_SIZE)
    scores = jnp.einsum("sqhd,skd->shqk", query_all, key_one, preferred_element_type=F32)
    scores = scores / jnp.sqrt(F32(HEAD_SIZE))
    place = jnp.arange(SEQUENCE_SLOTS, dtype=jnp.int32)
    rows = place[None, :, None]
    cols = place[None, None, :]
    inside = (cols >= offsets[:, None, None]) & (cols < lengths[:, None, None]) & (cols <= rows)
    visible = (inside | (cols == rows))[:, None, :, :]
    scores = jnp.where(visible, scores, F32(-1e30))
    top = jnp.max(scores, axis=-1, keepdims=True)
    expo = jnp.where(visible, jnp.exp(scores - top), F32(0.0))
    probs = (expo / jnp.sum(expo, axis=-1, keepdims=True)).astype(BF16)
    attn = jnp.einsum("shqk,skd->sqhd", probs, value_one, preferred_element_type=F32)
    return attn.astype(BF16).reshape(seqs * SEQUENCE_SLOTS, local_heads * HEAD_SIZE)


def pick(array, index, axis=0):
    return lax.dynamic_index_in_dim(array, index, axis, keepdims=False)


def add_up(blocks):
    total = blocks[0].astype(F32)
    for block in blocks[1:]:
        total = total + block.astype(F32)
    return total


def move(array, major, mask):
    return lax.ppermute(array, BOTH, across(major, mask))


def sum_major(blocks, size):
    blocks = [blocks[0]] + [move(blocks[e], True, e) for e in (2, 1, 3)]
    return [add_up([block[q * size : (q + 1) * size] for block in blocks]) for q in range(SIDE)]


def gather_x(block, earlier=None):
    other = lax.ppermute(block, "gy", across_x((1, 3)))
    if earlier is not None:
        other = after(other, earlier)
    return [block, other, lax.ppermute(jnp.concatenate([block, other]), "gy", across_x((3, 1)))]


def halves(core, array, axis=0):
    return pick(array, core, axis), pick(array, 1 - core, axis)


def swap(array):
    return lax.ppermute(array, "gy", SWAP)


def in_three(sums):
    lanes = []
    for _ in range(3):
        rounded = lax.reduce_precision(sums, 8, 7)
        lanes.append(rounded.astype(BF16))
        sums = sums - rounded
    return jnp.pad(jnp.stack(lanes, axis=1), ((0, 0), (0, 128 - 3)))


def after(array, *earlier):
    return lax.optimization_barrier((array, earlier))[0]


SMEM = pl.BlockSpec(memory_space=pltpu.SMEM)
VMEM = pl.BlockSpec(memory_space=pltpu.VMEM)
HBM = pl.BlockSpec(memory_space=pltpu.HBM)


def fill(places, given, lhs, size):
    i = 0
    for ref in given:
        for row in range(0, ref.shape[0], size):
            at = pl.multiple_of(places[i] * size, size)
            lhs[pl.ds(at, size), :] = ref[row : row + size, :]
            i += 1


def start_all(sources, targets, sems):
    copies = []
    for source, target in zip(sources, targets):
        piece = source.shape[0] // PIECES
        for j in range(PIECES):
            at = pl.ds(j * piece, piece)
            copies.append(
                pltpu.make_async_copy(source.at[at], target.at[at], sems.at[len(copies)])
            )
    for copy in copies:
        copy.start()
    return copies


def load(*weights):
    count = len(weights)

    def kernel(*refs):
        for copy in start_all(refs[:count], refs[count : 2 * count], refs[-1]):
            copy.wait()

    return pl.pallas_call(
        kernel,
        in_specs=[HBM] * count,
        out_specs=[VMEM] * count,
        scratch_shapes=[pltpu.SemaphoreType.DMA((count * PIECES,))],
        out_shape=[jax.ShapeDtypeStruct(weight.shape, BF16) for weight in weights],
        compiler_params=pltpu.CompilerParams(vmem_limit_bytes=PROJECT_BYTES),
        cost_estimate=pl.CostEstimate(
            flops=0, bytes_accessed=sum(2 * weight.size for weight in weights), transcendentals=0
        ),
    )(*weights)


def project(places, size, blocks, weight):
    depth, width = weight.shape
    rows = size * places.shape[0]

    def kernel(places, *refs):
        given, weight_ref, outs, lhs = refs[: len(blocks)], refs[-6], refs[-5:-1], refs[-1]
        fill(places, given, lhs, size)
        for first in range(0, width, TILE):
            at = pl.ds(first, TILE)
            product = jnp.dot(lhs[...], weight_ref[:, at], preferred_element_type=F32).astype(BF16)
            for e in range(4):
                outs[e][:, at] = product[e * rows // 4 : (e + 1) * rows // 4]

    return pl.pallas_call(
        kernel,
        in_specs=[SMEM] + [VMEM] * (len(blocks) + 1),
        out_specs=[VMEM] * 4,
        scratch_shapes=[pltpu.VMEM((rows, depth), BF16)],
        out_shape=[jax.ShapeDtypeStruct((rows // 4, width), BF16)] * 4,
        compiler_params=pltpu.CompilerParams(vmem_limit_bytes=PROJECT_BYTES),
        cost_estimate=pl.CostEstimate(
            flops=2 * rows * depth * width, bytes_accessed=2 * depth * width, transcendentals=0
        ),
    )(places, *blocks, weight)


def gate_and_up(places, blocks, w_gate, w_up):
    depth, units = w_gate.shape
    rows = blocks[0].shape[0]
    full = units // WIDE
    rest = units - full * WIDE

    def kernel(places, *refs):
        given, gate_ref, up_ref, outs = refs[:4], refs[4], refs[5], refs[6:8]
        lhs, tile_refs, sems = refs[8:]

        def copy(weight_ref, j, first):
            at = pl.ds(pl.multiple_of(j * WIDE, WIDE), WIDE)
            return pltpu.make_async_copy(
                weight_ref.at[:, at], tile_refs.at[first + j], sems.at[first + j]
            )

        def copy_rest(weight_ref, i):
            return pltpu.make_async_copy(
                weight_ref.at[:, pl.ds(full * WIDE, rest)],
                tile_refs.at[2 * full, :, pl.ds(i * rest, rest)],
                sems.at[2 * full + i],
            )

        def store(product, at):
            for i in range(2):
                outs[i][:, at] = product[2 * i * rows : 2 * (i + 1) * rows]

        def multiply(tile):
            return jnp.dot(lhs[:, :depth], tile, preferred_element_type=F32).astype(BF16)

        for j in range(AHEAD):
            copy(gate_ref, j, 0).start()
        fill(places, given, lhs, rows)
        store(lhs[:, depth:], pl.ds(2 * units, 128))

        @pl.loop(0, full)
        def _(j):
            copy(gate_ref, j, 0).wait()

            @pl.when(j + AHEAD < full)
            def _():
                copy(gate_ref, j + AHEAD, 0).start()

            @pl.when(j + AHEAD >= full)
            def _():
                copy(up_ref, j + AHEAD - full, full).start()

            at = pl.multiple_of(j * WIDE, WIDE)
            store(multiply(tile_refs[j]), pl.ds(at, WIDE))

        @pl.loop(0, full)
        def _(j):
            copy(up_ref, j, full).wait()

            @pl.when(j + AHEAD < full)
            def _():
                copy(up_ref, j + AHEAD, full).start()

            @pl.when(j + AHEAD == full)
            def _():
                copy_rest(gate_ref, 0).start()
                copy_rest(up_ref, 1).start()

            at = pl.multiple_of(units + j * WIDE, 128)
            store(multiply(tile_refs[full + j]), pl.ds(at, WIDE))

        copy_rest(gate_ref, 0).wait()
        copy_rest(up_ref, 1).wait()
        product = multiply(tile_refs[2 * full, :, : 2 * rest])
        store(product[:, :rest], pl.ds(full * WIDE, rest))
        store(product[:, rest:], pl.ds(units + full * WIDE, rest))

    return pl.pallas_call(
        kernel,
        in_specs=[SMEM] + [VMEM] * 4 + [HBM] * 2,
        out_specs=[VMEM] * 2,
        scratch_shapes=[
            pltpu.VMEM((4 * rows, depth + 128), BF16),
            pltpu.VMEM((2 * full + 1, depth, WIDE), BF16),
            pltpu.SemaphoreType.DMA((2 * full + 2,)),
        ],
        out_shape=[jax.ShapeDtypeStruct((2 * rows, 2 * units + 128), BF16)] * 2,
        compiler_params=pltpu.CompilerParams(vmem_limit_bytes=VMEM_BYTES),
        cost_estimate=pl.CostEstimate(
            flops=16 * rows * depth * units, bytes_accessed=4 * depth * units, transcendentals=0
        ),
    )(places, *blocks, w_gate, w_up)


def sum_over_x(sent, kept, earlier):
    rows = sent.shape[0] // 2
    arrived = after(lax.ppermute(sent, "gy", across_x((3, 1))), earlier)
    other = (kept[rows:].astype(F32) + arrived[rows:].astype(F32)).astype(BF16)
    other = lax.ppermute(other, "gy", across_x((1, 3)))
    return add_up([kept[:rows], arrived[:rows], other])


def per_device(
    queries, keys, values, lengths, offsets, resid_in, w_out, norm_gain, w_gate, w_up, w_down
):
    place = lax.axis_index("gx")
    y, z = place // SIDE, place % SIDE
    x, core = lax.axis_index("gy") // 2, lax.axis_index("gy") % 2
    here, there = jnp.where(core == 0, z, y), jnp.where(core == 0, y, z)
    rows, columns = resid_in.shape
    half = rows // 2
    units = w_gate.shape[1]
    four = jnp.arange(SIDE, dtype=jnp.int32)
    two = jnp.arange(2, dtype=jnp.int32)
    cores = jnp.stack([core, 1 - core])

    w_gate = lax.all_gather(w_gate, "gy", axis=0, tiled=True, axis_index_groups=CORES)
    w_up = lax.all_gather(w_up, "gy", axis=0, tiled=True, axis_index_groups=CORES)

    mine = attend_local(queries, keys, values, lengths, offsets)
    (out_weight,) = load(after(w_out, mine))
    mine = gather_x(mine, out_weight)
    theirs = swap(jnp.concatenate(mine))
    near = jnp.where(core == 0, 1, 3)
    zero, far = jnp.zeros_like(near), jnp.full_like(near, 2)
    lines = x ^ jnp.stack(
        [
            jnp.stack([zero, near, 4 - near, far]),
            jnp.stack([zero, 4 - near, near, far]),
        ]
    )
    in_y = (lines ^ y)[:, :, None]
    in_z = ((2 * cores[:, None] + two[None, :]) ^ z)[:, None, :]
    places = jnp.where(core == 0, 4 * in_z + in_y, 4 * in_y + in_z).reshape(16)
    parts = sum_major(project(places, rows, mine + [theirs], out_weight), rows)
    arrived = [move(parts[q].astype(BF16), False, q) for q in (2, 1, 3)]
    attn_proj = add_up([parts[0]] + arrived)
    wide = (resid_in.astype(F32) + attn_proj).astype(BF16).astype(F32)
    squares = in_three(jnp.sum(wide * wide, axis=1))
    scaled = jnp.concatenate([(wide * norm_gain.astype(F32)).astype(BF16), squares], axis=1)
    mine, theirs = halves(core, scaled.reshape(2, half, -1))
    theirs = swap(theirs)
    first, second = jnp.where(core == 0, mine, theirs), jnp.where(core == 0, theirs, mine)
    squares = mine[:, columns:].astype(F32) + theirs[:, columns:].astype(F32)
    scaled = jnp.concatenate(
        [first[:, :columns], second[:, :columns], in_three(jnp.sum(squares, axis=1))], axis=1
    )
    scaled = [scaled] + [move(scaled, False, q) for q in (1, 2, 3)]

    quarter = half // 2
    slot = x ^ here ^ four
    slots = jnp.where(slot == 4 - near, 0, jnp.where(slot == 2, 1, jnp.where(slot == 0, 2, 3)))
    products = []
    for chunk in range(2):
        taken = slice(chunk * quarter, (chunk + 1) * quarter)
        block = jnp.concatenate([block[taken] for block in scaled])
        blocks = [block] + [move(block, True, e) for e in (1, 2, 3)]
        products.append(gate_and_up(slots, blocks, w_gate, w_up))
    outs, placed = [], None
    for chunk, (sent, kept) in enumerate(products):
        both = sum_over_x(sent, kept, hidden if chunk else products[1][0])
        if not chunk:
            (down_weight,) = load(after(w_down, products[1][0]))
            both = after(both, down_weight)
        scale = lax.rsqrt(jnp.sum(both[:, 2 * units :], axis=1, keepdims=True) / D + 1e-05)
        gate, up = both[:, :units] * scale, both[:, units : 2 * units] * scale
        hidden = (jax.nn.silu(gate) * up).astype(BF16)
        mine = gather_x(hidden)
        if chunk:
            mine = after(mine, *placed)
        theirs = swap(jnp.concatenate(mine))
        ours = 4 * (lines[0] ^ here)[:, None] + four[None, :]
        others = (lines[1] ^ there)[:, None] + 4 * four[None, :]
        places = jnp.stack([2 * ours + core, 2 * others + 1 - core]).reshape(32)
        placed = project(places, quarter, mine + [theirs], down_weight)
        parts = sum_major(placed, half)
        arrived = [move(parts[q].astype(BF16), False, q) for q in (2, 1, 3)]
        own = wide.reshape(2, 2, quarter, columns)[:, chunk].reshape(half, columns)
        outs.append((own + add_up([parts[0]] + arrived)).astype(BF16).reshape(2, quarter, columns))
    return jnp.stack(outs, axis=1).reshape(rows, columns)


def solution(mesh):
    in_specs = (
        P("gy", "gx"),
        P("gy", None),
        P("gy", None),
        P("gy"),
        P("gy"),
        P("gx", "gy"),
        P("gx", "gy"),
        P("gy"),
        P("gy", "gx"),
        P("gy", "gx"),
        P("gx", "gy"),
    )
    out_specs = P("gx", "gy")
    return jax.shard_map(
        per_device, mesh=mesh, in_specs=in_specs, out_specs=out_specs, check_vma=False
    )
```
